32 devices in a mesh: ctx: 16 (over z, y, x), head: 2 (over core).
Axes of the slice: x: 2, y: 2, z: 4, core: 2. Of those that a mesh axis runs over, the one named last changes fastest.
Arguments:
- queries: bfloat16 [4096, 1024], P('ctx', 'head'), may hold values from -4 to 4
- key_rows: bfloat16 [4096, 1024], P('ctx', 'head'), may hold values from -4 to 4
- value_rows: bfloat16 [4096, 1024], P('ctx', 'head'), may hold values from -6 to 6
- out_grad: bfloat16 [4096, 1024], P('ctx', 'head'), may hold values from -6 to 6
- offsets: int32 [3, 4], P(None, 'head'), may hold values from 0 to 63
Outputs:
- query_grad: bfloat16 [4096, 1024], P('ctx', 'head')
- key_grad: bfloat16 [4096, 1024], P('ctx', 'head')
- value_grad: bfloat16 [4096, 1024], P('ctx', 'head')
The draws below stay inside these ranges and needn't reach their ends.
All inputs are finite; a program needn't handle non-finite values.
Results may differ from the reference program's by a relative error of at most 0.0068.
Values may be sent and summed in bfloat16 or wider, within the bound.
A program may use at most 128 MiB of HBM per device.

```python
import jax
import jax.numpy as jnp
from jax import lax

HEADS = 4
HD = 256
LEVELS = 3
R0 = 1
R1 = 16
R2 = 64
W0 = 2048
W1 = 32768
TOKENS = 4096


def draw_queries(key, part):
    key = jax.random.fold_in(key, 11)
    return jnp.clip(jax.random.normal(key, (TOKENS, HEADS * HD), jnp.float32), -4.0, 4.0).astype(jnp.bfloat16)


def draw_key_rows(key, part):
    key = jax.random.fold_in(key, 23)
    return jnp.clip(jax.random.normal(key, (TOKENS, HEADS * HD), jnp.float32), -4.0, 4.0).astype(jnp.bfloat16)


def plant(entries, key, smallest, top_value):
    dims = entries.shape
    index_at = [jax.random.randint(jax.random.fold_in(key, axis), (), 0, dims[axis]) for axis in range(len(dims))]
    entries = entries.at[tuple(index_at)].set(smallest)
    longest = dims.index(max(dims))
    index_at[longest] = (index_at[longest] + 1) % dims[longest]
    return entries.at[tuple(index_at)].set(top_value)


def shard_levels(own_key, extent, cuts, smallest, high):
    loudness, own = 1.0, jax.random.fold_in(own_key, 6)
    for dim, parts in cuts:
        draws = jnp.exp(jax.random.uniform(jax.random.fold_in(own, dim), (parts,), jnp.float32, smallest / len(cuts), high / len(cuts)))
        loudness = loudness * jnp.repeat(draws, extent[dim] // parts).reshape([-1 if axis == dim else 1 for axis in range(len(extent))])
    return loudness


def gaussian(own_key, extent, scale, bound, pieces=(), held_as=jnp.bfloat16):
    gain = shard_levels(own_key, extent, pieces, -0.22, 0.18) if pieces else 1.0
    result = jax.random.normal(own_key, extent, jnp.float32) * scale * gain
    return jnp.minimum(jnp.maximum(result, -bound), bound).astype(held_as)


def setup_inputs(seed: int = 0) -> dict:
    splits = jax.random.split(jax.random.key(seed), 6)
    queries = draw_queries(jax.random.fold_in(splits[5], 71), 0)
    key_rows = draw_key_rows(jax.random.fold_in(splits[5], 71), 0)
    value_rows = gaussian(splits[2], (TOKENS, HEADS * HD), 1.0, 6.0, ((0, 16), (1, 2)))
    out_grad = gaussian(splits[3], (TOKENS, HEADS * HD), 1.0, 6.0, ((0, 16), (1, 2)))
    offsets = plant(jax.random.randint(splits[4], (LEVELS, HEADS), 0, R2), jax.random.fold_in(splits[4], 1), 0, R2 - 1).astype(jnp.int32)
    return dict(queries=queries, key_rows=key_rows, value_rows=value_rows, out_grad=out_grad, offsets=offsets)


NEGATIVE = -1.0e30


def pick_rows(field, offset_row, rate):
    folded = field.reshape((field.shape[0] // rate, rate) + field.shape[1:])
    chosen = jnp.arange(rate, dtype=jnp.int32)[:, None] == (offset_row % rate)[None, :]
    chosen = chosen.reshape((1, rate, offset_row.shape[0]) + (1,) * (field.ndim - 2))
    return jnp.sum(jnp.where(chosen, folded, jnp.zeros((), field.dtype)), axis=1)


def place_rows(selected, offset_row, rate, fill):
    chosen = jnp.arange(rate, dtype=jnp.int32)[:, None] == (offset_row % rate)[None, :]
    chosen = chosen.reshape((1, rate, offset_row.shape[0]) + (1,) * (selected.ndim - 2))
    spread = jnp.where(chosen, selected[:, None], jnp.asarray(fill, selected.dtype))
    return spread.reshape((selected.shape[0] * rate,) + selected.shape[1:])


def segment_scores(query_seg, key_seg, scale):
    return jnp.einsum("qhd,khd->hqk", query_seg.astype(jnp.float32), key_seg.astype(jnp.float32)) * scale


def lowered(field):
    return lax.optimization_barrier(field.astype(jnp.bfloat16)).astype(jnp.float32)


def reference(queries, key_rows, value_rows, out_grad, offsets):
    scale = HD ** -0.5
    query_all = queries.reshape(TOKENS, HEADS, HD)
    key_all = key_rows.reshape(TOKENS, HEADS, HD)
    value_all = value_rows.reshape(TOKENS, HEADS, HD)
    grad_all = out_grad.reshape(TOKENS, HEADS, HD)
    rates = (R0, R1, R2)
    widths = (min(W0, TOKENS), min(W1, TOKENS), TOKENS)

    def forward(blocks):
        query_seg, key_seg, value_seg = blocks
        scores = segment_scores(query_seg, key_seg, scale)
        row_max = jnp.max(scores, axis=2)
        weights = jnp.exp(scores - row_max[:, :, None])
        row_sum = jnp.sum(weights, axis=2)
        partial_value = jnp.einsum("hqk,khd->qhd", lowered(weights), value_seg.astype(jnp.float32))
        return row_max.T, row_sum.T, partial_value

    maxima, sums, partials = [], [], []
    for level_no in range(LEVELS):
        rate, width = rates[level_no], widths[level_no]
        seg_rows, segs = width // rate, TOKENS // width
        picked = tuple(pick_rows(field, offsets[level_no], rate).reshape(segs, seg_rows, HEADS, HD)
                       for field in (query_all, key_all, value_all))
        row_max, row_sum, partial_value = lax.map(forward, picked)
        maxima.append(place_rows(row_max.reshape(TOKENS // rate, HEADS), offsets[level_no], rate, NEGATIVE))
        sums.append(place_rows(row_sum.reshape(TOKENS // rate, HEADS), offsets[level_no], rate, 0.0))
        partials.append(place_rows(partial_value.reshape(TOKENS // rate, HEADS, HD), offsets[level_no], rate, 0.0))
    top = maxima[0]
    for level_no in range(1, LEVELS):
        top = jnp.maximum(top, maxima[level_no])
    total = jnp.zeros((TOKENS, HEADS), jnp.float32)
    for level_no in range(LEVELS):
        total = total + jnp.exp(maxima[level_no] - top) * sums[level_no]
    lse = top + jnp.log(total)
    combined = jnp.zeros((TOKENS, HEADS, HD), jnp.float32)
    for level_no in range(LEVELS):
        combined = combined + jnp.exp(maxima[level_no] - lse)[:, :, None] * partials[level_no]
    delta = jnp.sum(grad_all.astype(jnp.float32) * combined, axis=2)

    def backward(blocks):
        query_seg, key_seg, value_seg, grad_seg, lse_seg, delta_seg = blocks
        scores = segment_scores(query_seg, key_seg, scale)
        probs = jnp.exp(scores - lse_seg.T[:, :, None])
        dprob = jnp.einsum("qhd,khd->hqk", grad_seg.astype(jnp.float32), value_seg.astype(jnp.float32))
        dscore = lowered(probs * (dprob - delta_seg.T[:, :, None]))
        dquery = jnp.einsum("hqk,khd->qhd", dscore, key_seg.astype(jnp.float32)) * scale
        dkey = jnp.einsum("hqk,qhd->khd", dscore, query_seg.astype(jnp.float32)) * scale
        dvalue = jnp.einsum("hqk,qhd->khd", lowered(probs), grad_seg.astype(jnp.float32))
        return dquery, dkey, dvalue

    grads = [jnp.zeros((TOKENS, HEADS, HD), jnp.float32) for _ in range(3)]
    for level_no in range(LEVELS):
        rate, width = rates[level_no], widths[level_no]
        seg_rows, segs = width // rate, TOKENS // width
        picked = tuple(pick_rows(field, offsets[level_no], rate).reshape(segs, seg_rows, HEADS, HD)
                       for field in (query_all, key_all, value_all, grad_all))
        stats = tuple(pick_rows(field, offsets[level_no], rate).reshape(segs, seg_rows, HEADS)
                      for field in (lse, delta))
        results = lax.map(backward, picked + stats)
        for slot_no in range(3):
            grads[slot_no] = grads[slot_no] + place_rows(
                results[slot_no].reshape(TOKENS // rate, HEADS, HD), offsets[level_no], rate, 0.0)
    return tuple(field.reshape(TOKENS, HEADS * HD).astype(jnp.bfloat16) for field in grads)
```

```python
import functools
import math

import jax
import jax.numpy as jnp
from jax import lax
from jax.experimental import pallas as pl
from jax.experimental.pallas import tpu as pltpu
from jax.sharding import PartitionSpec as P

HD = 256
R1 = 16
R2 = 64
W0 = 2048
PICK = 32
NEGATIVE = -1e30
SCALE = HD ** (-0.5)
LOG2 = SCALE * math.log2(math.e)
F32 = jnp.float32
BF16 = jnp.bfloat16


def dot_nt(a, b):
    return lax.dot_general(a, b, (((1,), (1,)), ((), ())), preferred_element_type=F32)


def dot_tn(a, b):
    return lax.dot_general(a, b, (((0,), (0,)), ((), ())), preferred_element_type=F32)


def dot_nn(a, b):
    return jnp.dot(a, b, preferred_element_type=F32)


def kernel(
    cubes, far_bits,
    q_ref, k_ref, v_ref, g_ref, off_ref,
    dq_ref, dk_ref, dv_ref,
    qb, gb, kb, vb, picks, pick_stage, stat_mine, stat_peer,
    e_buf, d_buf, ds_buf,
    kv_stage, kv_peer, kv_own, pk_stage, pk_peer, pk_own, far_stage, far_peer,
    q_stage, q_peer, q_own, fin,
    send_sem, recv_sem,
):
    rows = q_ref.shape[0]
    span = 4 * rows
    wide = cubes * 2 * PICK
    me = lax.axis_index("ctx")

    def bit(n):
        return lax.rem(lax.div(me, 1 << n), 2)

    def peer(n):
        return {"ctx": me + (1 << n) * (1 - 2 * bit(n))}

    x, y, z = bit(0), bit(1), bit(2)
    cube = lax.div(me, 8)
    used = []

    def send(src, dst, n):
        slot = len(used)
        copy = pltpu.make_async_remote_copy(
            src_ref=src, dst_ref=dst, send_sem=send_sem.at[slot], recv_sem=recv_sem.at[slot],
            device_id=peer(n), device_id_type=pl.DeviceIdType.MESH,
        )
        copy.start()
        used.append(copy)
        return copy

    def block(a, b):
        return pl.ds(pl.multiple_of((a * 2 + b) * rows, rows), rows)

    def cols(a):
        return pl.ds(pl.multiple_of(a * HD, HD), HD)

    barrier = pltpu.get_barrier_semaphore()
    for n in range(3 + far_bits):
        pl.semaphore_signal(barrier, inc=1, device_id=peer(n), device_id_type=pl.DeviceIdType.MESH)

    def offset(level, head):
        return jnp.where(head == 0, off_ref[level, 0], off_ref[level, 1])

    def one_hot(head, shape, row_dim):
        j = lax.broadcasted_iota(jnp.int32, shape, row_dim)
        p = lax.broadcasted_iota(jnp.int32, shape, 1 - row_dim)
        first = (j < 16) & (p == R1 * j + offset(0, head))
        second = (j >= 16) & (p == R2 * (j - 16) + offset(1, head))
        return jnp.where(first | second, 1.0, 0.0).astype(BF16)

    def head_of(ref, head):
        return jnp.where(head == 0, ref[:, :HD], ref[:, HD:])

    k_own, v_own = head_of(k_ref, z), head_of(v_ref, z)
    hot_other = one_hot(1 - z, (PICK, rows), 0)
    pick_stage[0] = dot_nn(hot_other, head_of(k_ref, 1 - z)).astype(BF16)
    pick_stage[1] = dot_nn(hot_other, head_of(v_ref, 1 - z)).astype(BF16)
    hot_mine = one_hot(z, (PICK, rows), 0)
    picks[x, 0, cube, z] = dot_nn(hot_mine, k_own).astype(BF16)
    picks[x, 1, cube, z] = dot_nn(hot_mine, v_own).astype(BF16)

    pl.semaphore_wait(barrier, 3 + far_bits)

    z_picks = send(pick_stage, picks.at[x, :, cube, z], 2)
    z_k = send(k_ref.at[:, cols(1 - z)], kb.at[block(x, z)], 2)
    x_k = send(k_ref.at[:, cols(z)], kb.at[block(x, z)], 0)
    y_q = send(q_ref.at[:, cols(z)], qb.at[block(y, z)], 1)
    z_q = send(q_ref.at[:, cols(1 - z)], qb.at[block(y, z)], 2)
    x_v = send(v_ref.at[:, cols(z)], vb.at[block(x, z)], 0)
    y_g = send(g_ref.at[:, cols(z)], gb.at[block(y, z)], 1)
    z_v = send(v_ref.at[:, cols(1 - z)], vb.at[block(x, z)], 2)
    z_g = send(g_ref.at[:, cols(1 - z)], gb.at[block(y, z)], 2)
    kb[block(x, z), :] = k_own
    vb[block(x, z), :] = v_own
    qb[block(y, z), :] = head_of(q_ref, z)
    gb[block(y, z), :] = head_of(g_ref, z)

    z_picks.wait_recv()
    for n in range(far_bits):
        group = pl.ds(lax.div(cube, 1 << n) * (1 << n), 1 << n)
        far = send(picks.at[x, :, group], picks.at[x, :, group], 3 + n)
        far.wait_recv()
    x_picks = send(picks.at[x], picks.at[x], 0)
    z_k.wait_recv()
    x_k2 = send(kb.at[block(x, 1 - z)], kb.at[block(x, 1 - z)], 0)
    z_q.wait_recv()
    y_q2 = send(qb.at[block(y, 1 - z)], qb.at[block(y, 1 - z)], 1)
    z_v.wait_recv()
    x_v2 = send(vb.at[block(x, 1 - z)], vb.at[block(x, 1 - z)], 0)
    z_g.wait_recv()
    y_g2 = send(gb.at[block(y, 1 - z)], gb.at[block(y, 1 - z)], 1)

    for copy in (x_picks, x_k, y_q, x_v, y_g, x_k2, y_q2, x_v2, y_g2):
        copy.wait_recv()

    def keys(c):
        return kb[c * rows:(c + 1) * rows, :] if c < 4 else picks[c - 4, 0].reshape(wide, HD)

    def values(c):
        return vb[c * rows:(c + 1) * rows, :] if c < 4 else picks[c - 4, 1].reshape(wide, HD)

    def place(c):
        return pl.ds(c * rows, rows) if c < 4 else pl.ds(span + (c - 4) * wide, wide)

    def forward(i, carry):
        here = pl.ds(pl.multiple_of(i * rows, rows), rows)
        q_now, g_now = qb[here, :], gb[here, :]
        j = lax.rem(lax.broadcasted_iota(jnp.int32, (wide, rows), 0), PICK)
        p = lax.broadcasted_iota(jnp.int32, (wide, rows), 1)
        mask = ((j < 16) & (lax.rem(p, R1) == offset(0, z))) | (
            (j >= 16) & (j < 16 + rows // R2) & (lax.rem(p, R2) == offset(1, z))
        )
        top = jnp.full((1, rows), NEGATIVE, F32)
        for c in range(6):
            s = dot_nt(keys(c), q_now) * LOG2
            if c >= 4:
                s = jnp.where(mask, s, NEGATIVE)
            e_buf[place(c), here] = s
            top = jnp.maximum(top, jnp.max(s, axis=0, keepdims=True))
        total = jnp.zeros((1, rows), F32)
        dotted = jnp.zeros((1, rows), F32)
        for c in range(6):
            e = jnp.exp2(e_buf[place(c), here] - top)
            d = dot_nt(values(c), g_now)
            e_buf[place(c), here] = e
            d_buf[place(c), here] = d
            total += jnp.sum(e, axis=0, keepdims=True)
            dotted += jnp.sum(e * d, axis=0, keepdims=True)
        stat_mine[:, here] = jnp.concatenate((top, total, dotted, jnp.zeros((5, rows), F32)), axis=0)
        return carry

    lax.fori_loop(0, 4, forward, 0)
    send(stat_mine, stat_peer, 1).wait_recv()
    top_a, top_b = stat_mine[0:1, :], stat_peer[0:1, :]
    top = jnp.maximum(top_a, top_b)
    keep_a, keep_b = jnp.exp2(top_a - top), jnp.exp2(top_b - top)
    inverse = 1.0 / (keep_a * stat_mine[1:2, :] + keep_b * stat_peer[1:2, :])
    factor = keep_a * inverse
    delta = (keep_a * stat_mine[2:3, :] + keep_b * stat_peer[2:3, :]) * inverse

    def backward(at):
        probs = e_buf[at, :] * factor
        dscore = (probs * (d_buf[at, :] - delta)).astype(BF16)
        ds_buf[at, :] = dscore
        return dot_nn(dscore, qb[...]) * SCALE, dot_nn(probs.astype(BF16), gb[...])

    def pick_at(a):
        return pl.ds(pl.multiple_of(span + a * wide, wide), wide)

    shape = (cubes, 2, PICK, HD)
    dk, dv = backward(pick_at(1 - x))
    pk_stage[0] = dk.astype(BF16).reshape(shape)
    pk_stage[1] = dv.astype(BF16).reshape(shape)
    x_pk = send(pk_stage, pk_peer, 0)
    x_kv = []
    for b in range(2):
        dk, dv = backward(block(1 - x, b))
        kv_stage[b, 0] = dk.astype(BF16)
        kv_stage[b, 1] = dv.astype(BF16)
        x_kv.append(send(kv_stage.at[b], kv_peer.at[b], 0))
    dk, dv = backward(pick_at(x))
    pk_own[0] = dk.reshape(shape)
    pk_own[1] = dv.reshape(shape)
    for b in range(2):
        dk, dv = backward(block(x, b))
        kv_own[b, 0] = dk
        kv_own[b, 1] = dv

    def dquery(a):
        at = pl.ds(pl.multiple_of(a * 2 * rows, 2 * rows), 2 * rows)
        total = dot_tn(ds_buf[pl.ds(0, span), at], kb[...])
        for c in (4, 5):
            total += dot_tn(ds_buf[place(c), at], keys(c))
        return total * SCALE

    q_stage[...] = dquery(1 - y).astype(BF16)
    y_dq = send(q_stage, q_peer, 1)
    q_own[...] = dquery(y)

    x_pk.wait_recv()
    pk_own[...] += pk_peer[...].astype(F32)
    for n in reversed(range(far_bits)):
        size = 1 << n
        mine = pl.ds(lax.div(cube, size) * size, size)
        low = lax.div(cube, 2 * size) * 2 * size
        other = pl.ds(low + (1 - bit(3 + n)) * size, size)
        far_stage[:, other] = pk_own[:, other].astype(BF16)
        far = send(far_stage.at[:, other], far_peer.at[n, :, pl.ds(0, size)], 3 + n)
        far.wait_recv()
        pk_own[:, mine] += far_peer[n, :, 0:size].astype(F32)

    spread = one_hot(z, (rows, PICK), 1)

    def final(kind, b):
        return kv_own[b, kind] + kv_peer[b, kind].astype(F32) + dot_nn(
            spread, pk_own[kind, cube, b].astype(BF16)
        )

    def final_q(b):
        at = pl.ds(pl.multiple_of(b * rows, rows), rows)
        return q_own[at, :] + q_peer[at, :].astype(F32)

    y_dq.wait_recv()
    fin[2] = final_q(1 - z).astype(BF16)
    last = [send(fin.at[2], dq_ref.at[:, cols(z)], 2)]
    x_kv[0].wait_recv()
    x_kv[1].wait_recv()
    for kind, out in ((0, dk_ref), (1, dv_ref)):
        fin[kind] = final(kind, 1 - z).astype(BF16)
        last.append(send(fin.at[kind], out.at[:, cols(z)], 2))
    dq_ref[:, cols(z)] = final_q(z).astype(BF16)
    dk_ref[:, cols(z)] = final(0, z).astype(BF16)
    dv_ref[:, cols(z)] = final(1, z).astype(BF16)
    for copy in last:
        copy.wait_recv()
    for copy in used:
        copy.wait_send()


def on_device(queries, key_rows, value_rows, out_grad, offsets):
    rows, columns = queries.shape
    axis_len = lax.axis_size("ctx")
    cubes = axis_len // 8
    far_bits = cubes.bit_length() - 1
    assert W0 // rows == 8 and columns == 2 * HD
    rates = jnp.array([[R1], [R2]], jnp.int32)
    offs = offsets[1:] % rates
    wide = cubes * 2 * PICK
    all_keys = 4 * rows + 2 * wide
    slots = 28 + 2 * far_bits
    out = jax.ShapeDtypeStruct((rows, columns), BF16)
    vmem = pl.BlockSpec(memory_space=pltpu.VMEM)
    held = pltpu.VMEM((4 * rows, HD), BF16)
    return pl.pallas_call(
        functools.partial(kernel, cubes, far_bits),
        out_shape=(out, out, out),
        in_specs=[vmem] * 4 + [pl.BlockSpec(memory_space=pltpu.SMEM)],
        out_specs=(vmem, vmem, vmem),
        scratch_shapes=[
            held, held, held, held,
            pltpu.VMEM((2, 2, cubes, 2, PICK, HD), BF16),
            pltpu.VMEM((2, PICK, HD), BF16),
            pltpu.VMEM((8, 4 * rows), F32),
            pltpu.VMEM((8, 4 * rows), F32),
            pltpu.VMEM((all_keys, 4 * rows), F32),
            pltpu.VMEM((all_keys, 4 * rows), F32),
            pltpu.VMEM((all_keys, 4 * rows), BF16),
            pltpu.VMEM((2, 2, rows, HD), BF16),
            pltpu.VMEM((2, 2, rows, HD), BF16),
            pltpu.VMEM((2, 2, rows, HD), F32),
            pltpu.VMEM((2, cubes, 2, PICK, HD), BF16),
            pltpu.VMEM((2, cubes, 2, PICK, HD), BF16),
            pltpu.VMEM((2, cubes, 2, PICK, HD), F32),
            pltpu.VMEM((2, cubes, 2, PICK, HD), BF16),
            pltpu.VMEM((far_bits, 2, cubes // 2, 2, PICK, HD), BF16),
            pltpu.VMEM((2 * rows, HD), BF16),
            pltpu.VMEM((2 * rows, HD), BF16),
            pltpu.VMEM((2 * rows, HD), F32),
            pltpu.VMEM((3, rows, HD), BF16),
            pltpu.SemaphoreType.DMA((slots,)),
            pltpu.SemaphoreType.DMA((slots,)),
        ],
        compiler_params=pltpu.CompilerParams(
            collective_id=0, has_side_effects=True, vmem_limit_bytes=60 * 1024 * 1024
        ),
    )(queries, key_rows, value_rows, out_grad, offs)


def solution(mesh):
    in_specs = (
        P("ctx", "head"),
        P("ctx", "head"),
        P("ctx", "head"),
        P("ctx", "head"),
        P(None, "head"),
    )
    out_specs = (P("ctx", "head"), P("ctx", "head"), P("ctx", "head"))
    return jax.shard_map(
        on_device, mesh=mesh, in_specs=in_specs, out_specs=out_specs, check_vma=False
    )
```

```python
import functools
import math

import jax
import jax.numpy as jnp
from jax import lax
from jax.experimental import pallas as pl
from jax.experimental.pallas import tpu as pltpu
from jax.sharding import PartitionSpec as P

HD = 256
R1 = 16
R2 = 64
W0 = 2048
PICK = 32
PARTS = 2
AHEAD = 3
NEGATIVE = -1e30
SCALE = HD ** (-0.5)
LOG2 = SCALE * math.log2(math.e)
F32 = jnp.float32
BF16 = jnp.bfloat16


def dot_nt(a, b):
    return lax.dot_general(a, b, (((1,), (1,)), ((), ())), preferred_element_type=F32)


def dot_tn(a, b):
    return lax.dot_general(a, b, (((0,), (0,)), ((), ())), preferred_element_type=F32)


def dot_nn(a, b):
    return jnp.dot(a, b, preferred_element_type=F32)


def kernel(
    cubes, far_bits,
    q_ref, k_ref, v_ref, g_ref, off_ref,
    dq_ref, dk_ref, dv_ref,
    qb, gb, kb, vb, picks, pick_stage, stat_mine, stat_peer,
    e_buf, d_buf, ds_buf,
    kv_stage, kv_peer, kv_own, pk_stage, pk_peer, pk_near, pk_own, far_stage, far_peer,
    q_stage, q_peer, q_own, fin,
    send_sem, recv_sem,
):
    rows = q_ref.shape[0]
    span = 4 * rows
    wide = cubes * 2 * PICK
    me = lax.axis_index("ctx")

    core = lax.axis_index("head")
    weights = (1 + core, 2 - core, 4) + tuple(8 << n for n in range(far_bits))

    def bit_of(n):
        return lax.rem(lax.div(me, weights[n]), 2)

    def peer(n):
        return {"ctx": me + weights[n] * (1 - 2 * bit_of(n))}

    x, y, z = bit_of(0), bit_of(1), bit_of(2)
    cube = lax.div(me, 8)
    used = []

    def send(src, dst, n):
        slot = len(used)
        copy = pltpu.make_async_remote_copy(
            src_ref=src, dst_ref=dst, send_sem=send_sem.at[slot], recv_sem=recv_sem.at[slot],
            device_id=peer(n), device_id_type=pl.DeviceIdType.MESH,
        )
        copy.start()
        used.append(copy)
        return copy

    def block(a, b):
        return pl.ds(pl.multiple_of((a * 2 + b) * rows, rows), rows)

    def cols(a):
        return pl.ds(pl.multiple_of(a * HD, HD), HD)

    barrier = pltpu.get_barrier_semaphore()
    for n in range(3 + far_bits):
        pl.semaphore_signal(barrier, inc=1, device_id=peer(n), device_id_type=pl.DeviceIdType.MESH)

    def offset(level, head):
        rate = (R1, R2)[level]
        return lax.rem(jnp.where(head == 0, off_ref[level + 1, 0], off_ref[level + 1, 1]), rate)

    def one_hot(head, shape, row_dim):
        j = lax.broadcasted_iota(jnp.int32, shape, row_dim)
        p = lax.broadcasted_iota(jnp.int32, shape, 1 - row_dim)
        first = (j < 16) & (p == R1 * j + offset(0, head))
        second = (j >= 16) & (p == R2 * (j - 16) + offset(1, head))
        return jnp.where(first | second, 1.0, 0.0).astype(BF16)

    def head_of(ref, head):
        return jnp.where(head == 0, ref[:, :HD], ref[:, HD:])

    k_own, v_own = head_of(k_ref, z), head_of(v_ref, z)
    hot_other = one_hot(1 - z, (PICK, rows), 0)
    pick_stage[0] = dot_nn(hot_other, head_of(k_ref, 1 - z)).astype(BF16)
    pick_stage[1] = dot_nn(hot_other, head_of(v_ref, 1 - z)).astype(BF16)
    hot_mine = one_hot(z, (PICK, rows), 0)
    picks[x, 0, cube, z] = dot_nn(hot_mine, k_own).astype(BF16)
    picks[x, 1, cube, z] = dot_nn(hot_mine, v_own).astype(BF16)

    pl.semaphore_wait(barrier, 3 + far_bits)

    part = rows // PARTS

    def piece(a, b, i):
        return pl.ds(pl.multiple_of((a * 2 + b) * rows + i * part, part), part)

    sources = ((k_ref, kb, x, 0), (q_ref, qb, y, 1), (v_ref, vb, x, 0), (g_ref, gb, y, 1))
    order = [(pair + kind, i) for pair in (0, 2) for i in range(PARTS) for kind in (0, 1)]

    def start_other(kind, i):
        ref, buf, a, _ = sources[kind]
        return send(ref.at[pl.ds(i * part, part), cols(1 - z)], buf.at[piece(a, z, i)], 2)

    def group(n, side):
        size = 1 << n
        low = lax.div(cube, 2 * size) * 2 * size
        mine = bit_of(3 + n)
        return pl.ds(low + (mine if side else 1 - mine) * size, size)

    z_picks = send(pick_stage, picks.at[x, :, cube, z], 2)
    flying = [start_other(*order[n]) for n in range(AHEAD)]
    arrivals = []
    for ref, buf, a, n in sources:
        arrivals.append(send(ref.at[:, cols(z)], buf.at[block(a, z)], n))
    kb[block(x, z), :] = k_own
    vb[block(x, z), :] = v_own
    qb[block(y, z), :] = head_of(q_ref, z)
    gb[block(y, z), :] = head_of(g_ref, z)

    z_picks.wait_recv()
    far = []
    for n in range(far_bits):
        far.append(send(picks.at[x, :, group(n, True)], picks.at[x, :, group(n, True)], 3 + n))
        if n < far_bits - 1:
            far[n].wait_recv()
            arrivals.append(send(picks.at[x, :, group(n, False)], picks.at[x, :, group(n, False)], 0))
    for n, (kind, i) in enumerate(order):
        _, buf, a, link = sources[kind]
        flying[n].wait_recv()
        if n + AHEAD < len(order):
            flying.append(start_other(*order[n + AHEAD]))
        there = buf.at[piece(a, 1 - z, i)]
        arrivals.append(send(there, there, link))
        if n == 1:
            n = far_bits - 1
            far[n].wait_recv()
            arrivals.append(send(picks.at[x, :, group(n, False)], picks.at[x, :, group(n, False)], 0))

    for copy in arrivals:
        copy.wait_recv()
    for b in range(2):
        picks[1 - x, 0, cube, b] = dot_nn(hot_mine, kb[block(1 - x, b), :]).astype(BF16)
        picks[1 - x, 1, cube, b] = dot_nn(hot_mine, vb[block(1 - x, b), :]).astype(BF16)

    def keys(c):
        return kb[c * rows:(c + 1) * rows, :] if c < 4 else picks[c - 4, 0].reshape(wide, HD)

    def values(c):
        return vb[c * rows:(c + 1) * rows, :] if c < 4 else picks[c - 4, 1].reshape(wide, HD)

    def place(c):
        return pl.ds(c * rows, rows) if c < 4 else pl.ds(span + (c - 4) * wide, wide)

    def forward(i, carry):
        here = pl.ds(pl.multiple_of(i * rows, rows), rows)
        q_now, g_now = qb[here, :], gb[here, :]
        j = lax.rem(lax.broadcasted_iota(jnp.int32, (wide, rows), 0), PICK)
        p = lax.broadcasted_iota(jnp.int32, (wide, rows), 1)
        mask = ((j < 16) & (lax.rem(p, R1) == offset(0, z))) | (
            (j >= 16) & (j < 16 + rows // R2) & (lax.rem(p, R2) == offset(1, z))
        )
        top = jnp.full((1, rows), NEGATIVE, F32)
        for c in range(6):
            s = dot_nt(keys(c), q_now) * LOG2
            if c >= 4:
                s = jnp.where(mask, s, NEGATIVE)
            e_buf[place(c), here] = s
            top = jnp.maximum(top, jnp.max(s, axis=0, keepdims=True))
        total = jnp.zeros((1, rows), F32)
        dotted = jnp.zeros((1, rows), F32)
        for c in range(6):
            e = jnp.exp2(e_buf[place(c), here] - top)
            d = dot_nt(values(c), g_now)
            e_buf[place(c), here] = e
            d_buf[place(c), here] = d
            total += jnp.sum(e, axis=0, keepdims=True)
            dotted += jnp.sum(e * d, axis=0, keepdims=True)
        stat_mine[:, here] = jnp.concatenate((top, total, dotted, jnp.zeros((5, rows), F32)), axis=0)
        return carry

    lax.fori_loop(0, 4, forward, 0)
    send(stat_mine, stat_peer, 1).wait_recv()
    top_a, top_b = stat_mine[0:1, :], stat_peer[0:1, :]
    top = jnp.maximum(top_a, top_b)
    keep_a, keep_b = jnp.exp2(top_a - top), jnp.exp2(top_b - top)
    inverse = 1.0 / (keep_a * stat_mine[1:2, :] + keep_b * stat_peer[1:2, :])
    factor = keep_a * inverse
    delta = (keep_a * stat_mine[2:3, :] + keep_b * stat_peer[2:3, :]) * inverse

    def backward(at):
        probs = e_buf[at, :] * factor
        dscore = (probs * (d_buf[at, :] - delta)).astype(BF16)
        ds_buf[at, :] = dscore
        return dot_nn(dscore, qb[...]) * SCALE, dot_nn(probs.astype(BF16), gb[...])

    def pick_at(a):
        return pl.ds(pl.multiple_of(span + a * wide, wide), wide)

    shape = (cubes, 2, PICK, HD)
    dk, dv = backward(pick_at(1 - x))
    pk_near[0] = dk.reshape(shape)
    pk_near[1] = dv.reshape(shape)
    x_pk = []
    for n in range(far_bits):
        there = group(n, False)
        pk_stage[:, there] = pk_near[:, there].astype(BF16)
        x_pk.append(send(pk_stage.at[:, there], pk_peer.at[:, there], 0))
    spread = one_hot(z, (rows, PICK), 1)
    x_kv = {}
    for name, b in ((1, 1 - z), (0, z)):
        for kind, grad in enumerate(backward(block(1 - x, b))):
            near = dot_nn(spread, pk_near[kind, cube, b].astype(BF16))
            kv_stage[b, kind] = (grad + near).astype(BF16)
            x_kv[name, kind] = send(kv_stage.at[b, kind], kv_peer.at[b, kind], 0)
    dk, dv = backward(pick_at(x))
    pk_own[0] = dk.reshape(shape)
    pk_own[1] = dv.reshape(shape)
    for b in (1 - z, z):
        dk, dv = backward(block(x, b))
        kv_own[b, 0] = dk
        kv_own[b, 1] = dv

    def dquery(a, b):
        at = block(a, b)
        total = dot_tn(ds_buf[pl.ds(0, span), at], kb[...])
        for c in (4, 5):
            total += dot_tn(ds_buf[place(c), at], keys(c))
        return total * SCALE

    y_dq = {}
    for name, b in ((1, 1 - z), (0, z)):
        q_stage[b] = dquery(1 - y, b).astype(BF16)
        y_dq[name] = send(q_stage.at[b], q_peer.at[b], 1)
    for b in (1 - z, z):
        q_own[b] = dquery(y, b)

    for n in range(far_bits):
        there = group(n, False)
        x_pk[n].wait_recv()
        pk_own[:, there] += pk_peer[:, there].astype(F32)
    for n in reversed(range(far_bits)):
        size = 1 << n
        mine, other = group(n, True), group(n, False)
        far_stage[:, other] = pk_own[:, other].astype(BF16)
        far = send(far_stage.at[:, other], far_peer.at[n, :, pl.ds(0, size)], 3 + n)
        far.wait_recv()
        pk_own[:, mine] += far_peer[n, :, 0:size].astype(F32)

    def final(kind, b):
        return kv_own[b, kind] + kv_peer[b, kind].astype(F32) + dot_nn(
            spread, pk_own[kind, cube, b].astype(BF16)
        )

    def final_q(b):
        return q_own[b] + q_peer[b].astype(F32)

    y_dq[1].wait_recv()
    fin[2] = final_q(1 - z).astype(BF16)
    last = [send(fin.at[2], dq_ref.at[:, cols(z)], 2)]
    for kind, out in ((0, dk_ref), (1, dv_ref)):
        x_kv[1, kind].wait_recv()
        fin[kind] = final(kind, 1 - z).astype(BF16)
        last.append(send(fin.at[kind], out.at[:, cols(z)], 2))
    y_dq[0].wait_recv()
    dq_ref[:, cols(z)] = final_q(z).astype(BF16)
    for kind, out in ((0, dk_ref), (1, dv_ref)):
        x_kv[0, kind].wait_recv()
        out[:, cols(z)] = final(kind, z).astype(BF16)
    for copy in last:
        copy.wait_recv()
    for copy in used:
        copy.wait_send()


def on_device(queries, key_rows, value_rows, out_grad, offsets):
    rows, columns = queries.shape
    axis_len = lax.axis_size("ctx")
    cubes = axis_len // 8
    far_bits = cubes.bit_length() - 1
    assert W0 // rows == 8 and columns == 2 * HD
    wide = cubes * 2 * PICK
    all_keys = 4 * rows + 2 * wide
    slots = 6 + 8 * PARTS + 8 + 8 + 4 * far_bits
    out = jax.ShapeDtypeStruct((rows, columns), BF16)
    vmem = pl.BlockSpec(memory_space=pltpu.VMEM)
    held = pltpu.VMEM((4 * rows, HD), BF16)
    return pl.pallas_call(
        functools.partial(kernel, cubes, far_bits),
        out_shape=(out, out, out),
        in_specs=[vmem] * 4 + [pl.BlockSpec(memory_space=pltpu.SMEM)],
        out_specs=(vmem, vmem, vmem),
        scratch_shapes=[
            held, held, held, held,
            pltpu.VMEM((2, 2, cubes, 2, PICK, HD), BF16),
            pltpu.VMEM((2, PICK, HD), BF16),
            pltpu.VMEM((8, 4 * rows), F32),
            pltpu.VMEM((8, 4 * rows), F32),
            pltpu.VMEM((all_keys, 4 * rows), F32),
            pltpu.VMEM((all_keys, 4 * rows), F32),
            pltpu.VMEM((all_keys, 4 * rows), BF16),
            pltpu.VMEM((2, 2, rows, HD), BF16),
            pltpu.VMEM((2, 2, rows, HD), BF16),
            pltpu.VMEM((2, 2, rows, HD), F32),
            pltpu.VMEM((2, cubes, 2, PICK, HD), BF16),
            pltpu.VMEM((2, cubes, 2, PICK, HD), BF16),
            pltpu.VMEM((2, cubes, 2, PICK, HD), F32),
            pltpu.VMEM((2, cubes, 2, PICK, HD), F32),
            pltpu.VMEM((2, cubes, 2, PICK, HD), BF16),
            pltpu.VMEM((far_bits, 2, cubes // 2, 2, PICK, HD), BF16),
            pltpu.VMEM((2, rows, HD), BF16),
            pltpu.VMEM((2, rows, HD), BF16),
            pltpu.VMEM((2, rows, HD), F32),
            pltpu.VMEM((3, rows, HD), BF16),
            pltpu.SemaphoreType.DMA((slots,)),
            pltpu.SemaphoreType.DMA((slots,)),
        ],
        compiler_params=pltpu.CompilerParams(
            collective_id=0, has_side_effects=True, vmem_limit_bytes=60 * 1024 * 1024
        ),
    )(queries, key_rows, value_rows, out_grad, offsets)


def solution(mesh):
    in_specs = (
        P("ctx", "head"),
        P("ctx", "head"),
        P("ctx", "head"),
        P("ctx", "head"),
        P(None, "head"),
    )
    out_specs = (P("ctx", "head"), P("ctx", "head"), P("ctx", "head"))
    return jax.shard_map(
        on_device, mesh=mesh, in_specs=in_specs, out_specs=out_specs, check_vma=False
    )
```

```python
import functools
import math

import jax
import jax.numpy as jnp
from jax import lax
from jax.experimental import pallas as pl
from jax.experimental.pallas import tpu as pltpu
from jax.sharding import PartitionSpec as P

HD = 256
R1 = 16
R2 = 64
W0 = 2048
PICK = 32
PARTS = 2
AHEAD = 3
FAR_AT = 5
BATCH = 2
NEGATIVE = -1e30
SCALE = HD ** (-0.5)
LOG2 = SCALE * math.log2(math.e)
F32 = jnp.float32
BF16 = jnp.bfloat16


def dot_nt(a, b):
    return lax.dot_general(a, b, (((1,), (1,)), ((), ())), preferred_element_type=F32)


def dot_tn(a, b):
    return lax.dot_general(a, b, (((0,), (0,)), ((), ())), preferred_element_type=F32)


def dot_nn(a, b):
    return jnp.dot(a, b, preferred_element_type=F32)


def kernel(
    cubes, far_bits,
    q_ref, k_ref, v_ref, g_ref, off_ref,
    dq_ref, dk_ref, dv_ref,
    qb, gb, kb, vb, picks, pick_stage, stat_mine, stat_peer,
    e_buf, d_buf, ds_buf,
    kv_stage, kv_peer, kv_own, pk_stage, pk_peer, pk_near, pk_own, far_stage, far_peer,
    q_stage, q_peer, q_own, fin,
    send_sem, recv_sem,
):
    rows = q_ref.shape[0]
    span = 4 * rows
    wide = cubes * 2 * PICK
    me = lax.axis_index("ctx")

    core = lax.axis_index("head")
    weights = (1 + core, 2 - core, 4) + tuple(8 << n for n in range(far_bits))

    def bit_of(n):
        return lax.rem(lax.div(me, weights[n]), 2)

    def peer(n):
        return {"ctx": me + weights[n] * (1 - 2 * bit_of(n))}

    x, y, z = bit_of(0), bit_of(1), bit_of(2)
    cube = lax.div(me, 8)
    used = []

    def send(src, dst, n):
        slot = len(used)
        copy = pltpu.make_async_remote_copy(
            src_ref=src, dst_ref=dst, send_sem=send_sem.at[slot], recv_sem=recv_sem.at[slot],
            device_id=peer(n), device_id_type=pl.DeviceIdType.MESH,
        )
        copy.start()
        used.append(copy)
        return copy

    def block(a, b):
        return pl.ds(pl.multiple_of((a * 2 + b) * rows, rows), rows)

    def cols(a):
        return pl.ds(pl.multiple_of(a * HD, HD), HD)

    barrier = pltpu.get_barrier_semaphore()
    for n in range(3 + far_bits):
        pl.semaphore_signal(barrier, inc=1, device_id=peer(n), device_id_type=pl.DeviceIdType.MESH)

    def offset(level, head):
        rate = (R1, R2)[level]
        return lax.rem(jnp.where(head == 0, off_ref[0, level + 1], off_ref[1, level + 1]), rate)

    def one_hot(head, shape, row_dim):
        j = lax.broadcasted_iota(jnp.int32, shape, row_dim)
        p = lax.broadcasted_iota(jnp.int32, shape, 1 - row_dim)
        first = (j < 16) & (p == R1 * j + offset(0, head))
        second = (j >= 16) & (p == R2 * (j - 16) + offset(1, head))
        return jnp.where(first | second, 1.0, 0.0).astype(BF16)

    def head_of(ref, head):
        return jnp.where(head == 0, ref[:, :HD], ref[:, HD:])

    k_own, v_own = head_of(k_ref, z), head_of(v_ref, z)
    hot_other = one_hot(1 - z, (PICK, rows), 0)
    pick_stage[0] = dot_nn(hot_other, head_of(k_ref, 1 - z)).astype(BF16)
    pick_stage[1] = dot_nn(hot_other, head_of(v_ref, 1 - z)).astype(BF16)
    hot_mine = one_hot(z, (PICK, rows), 0)
    picks[x, 0, cube, z] = dot_nn(hot_mine, k_own).astype(BF16)
    picks[x, 1, cube, z] = dot_nn(hot_mine, v_own).astype(BF16)

    pl.semaphore_wait(barrier, 3 + far_bits)

    part = rows // PARTS

    def piece(a, b, i):
        return pl.ds(pl.multiple_of((a * 2 + b) * rows + i * part, part), part)

    sources = ((k_ref, kb, x, 0), (q_ref, qb, y, 1), (v_ref, vb, x, 0), (g_ref, gb, y, 1))
    order = [(pair + kind, i) for pair in (0, 2) for i in range(PARTS) for kind in (0, 1)]

    def start_other(kind, i):
        ref, buf, a, _ = sources[kind]
        return send(ref.at[pl.ds(i * part, part), cols(1 - z)], buf.at[piece(a, z, i)], 2)

    def group(n, side):
        size = 1 << n
        low = lax.div(cube, 2 * size) * 2 * size
        mine = bit_of(3 + n)
        return pl.ds(low + (mine if side else 1 - mine) * size, size)

    z_picks = send(pick_stage, picks.at[x, :, cube, z], 2)
    flying = [start_other(*order[n]) for n in range(AHEAD)]
    arrivals = []
    for ref, buf, a, n in sources:
        arrivals.append(send(ref.at[:, cols(z)], buf.at[block(a, z)], n))
    kb[block(x, z), :] = k_own
    vb[block(x, z), :] = v_own
    qb[block(y, z), :] = head_of(q_ref, z)
    gb[block(y, z), :] = head_of(g_ref, z)

    z_picks.wait_recv()
    far = []
    for n in range(far_bits):
        far.append(send(picks.at[x, :, group(n, True)], picks.at[x, :, group(n, True)], 3 + n))
        if n < far_bits - 1:
            far[n].wait_recv()
            arrivals.append(send(picks.at[x, :, group(n, False)], picks.at[x, :, group(n, False)], 0))
    for n, (kind, i) in enumerate(order):
        _, buf, a, link = sources[kind]
        flying[n].wait_recv()
        if n + AHEAD < len(order):
            flying.append(start_other(*order[n + AHEAD]))
        there = buf.at[piece(a, 1 - z, i)]
        arrivals.append(send(there, there, link))
        if n == FAR_AT:
            n = far_bits - 1
            far[n].wait_recv()
            arrivals.append(send(picks.at[x, :, group(n, False)], picks.at[x, :, group(n, False)], 0))

    for copy in arrivals:
        copy.wait_recv()
    for b in range(2):
        picks[1 - x, 0, cube, b] = dot_nn(hot_mine, kb[block(1 - x, b), :]).astype(BF16)
        picks[1 - x, 1, cube, b] = dot_nn(hot_mine, vb[block(1 - x, b), :]).astype(BF16)

    def keys(c):
        return kb[c * rows:(c + 1) * rows, :] if c < 4 else picks[c - 4, 0].reshape(wide, HD)

    def values(c):
        return vb[c * rows:(c + 1) * rows, :] if c < 4 else picks[c - 4, 1].reshape(wide, HD)

    def place(c):
        return pl.ds(c * rows, rows) if c < 4 else pl.ds(span + (c - 4) * wide, wide)

    def forward(i, carry):
        here = pl.ds(pl.multiple_of(i * rows, rows), rows)
        q_now, g_now = qb[here, :], gb[here, :]
        j = lax.rem(lax.broadcasted_iota(jnp.int32, (wide, rows), 0), PICK)
        p = lax.broadcasted_iota(jnp.int32, (wide, rows), 1)
        mask = ((j < 16) & (lax.rem(p, R1) == offset(0, z))) | (
            (j >= 16) & (j < 16 + rows // R2) & (lax.rem(p, R2) == offset(1, z))
        )
        top = jnp.full((1, rows), NEGATIVE, F32)
        for c in range(6):
            s = dot_nt(keys(c), q_now) * LOG2
            if c >= 4:
                s = jnp.where(mask, s, NEGATIVE)
            e_buf[place(c), here] = s
            top = jnp.maximum(top, jnp.max(s, axis=0, keepdims=True))
        total = jnp.zeros((1, rows), F32)
        dotted = jnp.zeros((1, rows), F32)
        for c in range(6):
            e = jnp.exp2(e_buf[place(c), here] - top)
            d = dot_nt(values(c), g_now)
            e_buf[place(c), here] = e
            d_buf[place(c), here] = d
            total += jnp.sum(e, axis=0, keepdims=True)
            dotted += jnp.sum(e * d, axis=0, keepdims=True)
        stat_mine[:, here] = jnp.concatenate((top, total, dotted, jnp.zeros((5, rows), F32)), axis=0)
        return carry

    swaps = []
    for i in range(0, 4, BATCH):
        lax.fori_loop(i, i + BATCH, forward, 0)
        here = pl.ds(i * rows, BATCH * rows)
        swaps.append(send(stat_mine.at[:, here], stat_peer.at[:, here], 1))
    for copy in swaps:
        copy.wait_recv()
    top_a, top_b = stat_mine[0:1, :], stat_peer[0:1, :]
    top = jnp.maximum(top_a, top_b)
    keep_a, keep_b = jnp.exp2(top_a - top), jnp.exp2(top_b - top)
    inverse = 1.0 / (keep_a * stat_mine[1:2, :] + keep_b * stat_peer[1:2, :])
    factor = keep_a * inverse
    delta = (keep_a * stat_mine[2:3, :] + keep_b * stat_peer[2:3, :]) * inverse

    def backward(at):
        probs = e_buf[at, :] * factor
        dscore = (probs * (d_buf[at, :] - delta)).astype(BF16)
        ds_buf[at, :] = dscore
        return dot_nn(dscore, qb[...]) * SCALE, dot_nn(probs.astype(BF16), gb[...])

    def pick_at(a):
        return pl.ds(pl.multiple_of(span + a * wide, wide), wide)

    shape = (cubes, 2, PICK, HD)
    dk, dv = backward(pick_at(1 - x))
    pk_near[0] = dk.reshape(shape)
    pk_near[1] = dv.reshape(shape)
    x_pk = []
    for n in range(far_bits):
        there = group(n, False)
        pk_stage[:, there] = pk_near[:, there].astype(BF16)
        x_pk.append(send(pk_stage.at[:, there], pk_peer.at[:, there], 0))
    spread = one_hot(z, (rows, PICK), 1)
    x_kv = {}
    for name, b in ((1, 1 - z), (0, z)):
        for kind, grad in enumerate(backward(block(1 - x, b))):
            near = dot_nn(spread, pk_near[kind, cube, b].astype(BF16))
            kv_stage[b, kind] = (grad + near).astype(BF16)
            x_kv[name, kind] = send(kv_stage.at[b, kind], kv_peer.at[b, kind], 0)
    dk, dv = backward(pick_at(x))
    pk_own[0] = dk.reshape(shape)
    pk_own[1] = dv.reshape(shape)
    for n in range(far_bits):
        there = group(n, False)
        x_pk[n].wait_recv()
        pk_own[:, there] += pk_peer[:, there].astype(F32)

    def far_start(n):
        other = group(n, False)
        far_stage[:, other] = pk_own[:, other].astype(BF16)
        return send(far_stage.at[:, other], far_peer.at[n, :, pl.ds(0, 1 << n)], 3 + n)

    def far_end(n, copy):
        copy.wait_recv()
        pk_own[:, group(n, True)] += far_peer[n, :, 0:1 << n].astype(F32)

    far_first = far_start(far_bits - 1)
    for b in (1 - z, z):
        dk, dv = backward(block(x, b))
        kv_own[b, 0] = dk
        kv_own[b, 1] = dv

    def dquery(a, b):
        at = block(a, b)
        total = dot_tn(ds_buf[pl.ds(0, span), at], kb[...])
        for c in (4, 5):
            total += dot_tn(ds_buf[place(c), at], keys(c))
        return total * SCALE

    y_dq = {}
    for name, b in ((1, 1 - z), (0, z)):
        q_stage[b] = dquery(1 - y, b).astype(BF16)
        y_dq[name] = send(q_stage.at[b], q_peer.at[b], 1)
    for b in (1 - z, z):
        q_own[b] = dquery(y, b)

    def final(kind, b):
        return kv_own[b, kind] + kv_peer[b, kind].astype(F32) + dot_nn(
            spread, pk_own[kind, cube, b].astype(BF16)
        )

    def final_q(b):
        return q_own[b] + q_peer[b].astype(F32)

    y_dq[1].wait_recv()
    fin[2] = final_q(1 - z).astype(BF16)
    last = [send(fin.at[2], dq_ref.at[:, cols(z)], 2)]
    far_end(far_bits - 1, far_first)
    for n in reversed(range(far_bits - 1)):
        far_end(n, far_start(n))
    for kind, out in ((0, dk_ref), (1, dv_ref)):
        x_kv[1, kind].wait_recv()
        fin[kind] = final(kind, 1 - z).astype(BF16)
        last.append(send(fin.at[kind], out.at[:, cols(z)], 2))
    y_dq[0].wait_recv()
    dq_ref[:, cols(z)] = final_q(z).astype(BF16)
    for kind, out in ((0, dk_ref), (1, dv_ref)):
        x_kv[0, kind].wait_recv()
        out[:, cols(z)] = final(kind, z).astype(BF16)
    for copy in last:
        copy.wait_recv()
    for copy in used:
        copy.wait_send()


def settle_kernel(a_in, b_in, c_in, a_out, b_out, c_out):
    a_out[...] = a_in[...]
    b_out[...] = b_in[...]
    c_out[...] = c_in[...]


def settle(*grads):
    vmem = pl.BlockSpec(memory_space=pltpu.VMEM)
    return pl.pallas_call(
        settle_kernel,
        out_shape=tuple(jax.ShapeDtypeStruct(g.shape, g.dtype) for g in grads),
        in_specs=[vmem] * 3,
        out_specs=(vmem,) * 3,
    )(*grads)


def on_device(queries, key_rows, value_rows, out_grad, offsets):
    rows, columns = queries.shape
    axis_len = lax.axis_size("ctx")
    cubes = axis_len // 8
    far_bits = cubes.bit_length() - 1
    assert W0 // rows == 8 and columns == 2 * HD
    wide = cubes * 2 * PICK
    all_keys = 4 * rows + 2 * wide
    slots = 6 + 8 * PARTS + 8 + 8 + 4 * far_bits
    out = jax.ShapeDtypeStruct((rows, columns), BF16)
    vmem = pl.BlockSpec(memory_space=pltpu.VMEM)
    held = pltpu.VMEM((4 * rows, HD), BF16)
    grads = pl.pallas_call(
        functools.partial(kernel, cubes, far_bits),
        out_shape=(out, out, out),
        in_specs=[vmem] * 4 + [pl.BlockSpec(memory_space=pltpu.SMEM)],
        out_specs=(vmem, vmem, vmem),
        scratch_shapes=[
            held, held, held, held,
            pltpu.VMEM((2, 2, cubes, 2, PICK, HD), BF16),
            pltpu.VMEM((2, PICK, HD), BF16),
            pltpu.VMEM((8, 4 * rows), F32),
            pltpu.VMEM((8, 4 * rows), F32),
            pltpu.VMEM((all_keys, 4 * rows), F32),
            pltpu.VMEM((all_keys, 4 * rows), F32),
            pltpu.VMEM((all_keys, 4 * rows), BF16),
            pltpu.VMEM((2, 2, rows, HD), BF16),
            pltpu.VMEM((2, 2, rows, HD), BF16),
            pltpu.VMEM((2, 2, rows, HD), F32),
            pltpu.VMEM((2, cubes, 2, PICK, HD), BF16),
            pltpu.VMEM((2, cubes, 2, PICK, HD), BF16),
            pltpu.VMEM((2, cubes, 2, PICK, HD), F32),
            pltpu.VMEM((2, cubes, 2, PICK, HD), F32),
            pltpu.VMEM((2, cubes, 2, PICK, HD), BF16),
            pltpu.VMEM((far_bits, 2, cubes // 2, 2, PICK, HD), BF16),
            pltpu.VMEM((2, rows, HD), BF16),
            pltpu.VMEM((2, rows, HD), BF16),
            pltpu.VMEM((2, rows, HD), F32),
            pltpu.VMEM((3, rows, HD), BF16),
            pltpu.SemaphoreType.DMA((slots,)),
            pltpu.SemaphoreType.DMA((slots,)),
        ],
        compiler_params=pltpu.CompilerParams(
            collective_id=0, has_side_effects=True, vmem_limit_bytes=60 * 1024 * 1024
        ),
    )(queries, key_rows, value_rows, out_grad, offsets.T)
    return settle(*grads)


def solution(mesh):
    in_specs = (
        P("ctx", "head"),
        P("ctx", "head"),
        P("ctx", "head"),
        P("ctx", "head"),
        P(None, "head"),
    )
    out_specs = (P("ctx", "head"), P("ctx", "head"), P("ctx", "head"))
    return jax.shard_map(
        on_device, mesh=mesh, in_specs=in_specs, out_specs=out_specs, check_vma=False
    )
```
